32 devices in a mesh: seq: 32 (over z, y, x, core), mp: 1.
Axes of the slice: x: 2, y: 2, z: 4, core: 2. Of those that a mesh axis runs over, the one named last changes fastest.
Arguments:
- streams: float32 [4096, 3, 4096], P('seq', None, 'mp'), may hold values from -6 to 6
- se_filter: float32 [7, 3, 256], P(None, None, 'mp'), may hold values from -3 to 3
- mr_filter: float32 [128, 256], P(None, 'mp'), may hold values from -1.5 to 1.5
- mr_decay: float32 [256], P('mp'), may hold values from 0.004 to 0.1
- query: float32 [4096, 4096], P('seq', 'mp'), may hold values from -8 to 8
- key: float32 [4096, 4096], P('seq', 'mp'), may hold values from -8 to 8
- value: float32 [4096, 4096], P('seq', 'mp'), may hold values from -6 to 6
- placement_list: int32 [32], replicated, may hold values from 0 to 31, each once
- doc_ids: int32 [4096], replicated, may hold values from 0 to 7, never falling along the last dimension, each value on 1 to 1024 neighbouring positions
- norm_gain: float32 [4096], P('mp'), may hold values from 0.25 to 1.75
Outputs:
- mixed: float32 [4096, 4096], P('seq', 'mp')
The draws below stay inside these ranges and needn't reach their ends.
Inputs may be any that keep to these rules, and one draw needn't show every extreme that they name: placement_list names every stretch once. doc_ids never falls along the sequence; each document holds at most 1024 positions and one holds exactly that many.
All inputs are finite; a program needn't handle non-finite values.
Results may differ from the reference program's by a relative error of at most 0.0003.
Values sent between devices are 32-bit elements; how exact they have to be, the bound alone decides.
A program may use at most 576 MiB of HBM per device.

```python
import math
import jax
import jax.numpy as jnp
import numpy as np
from jax import lax

CH = 4096
GROUP = 16
GROUPS = 256
SE_LEN = 7
MR_LEN = 128
HEADS = 32
HD = 128
TOK_DEV = 128
TOKENS = 4096
DOCS = 8
N_SEQ = 32


def drawn_pair(key):
    shape = (TOKENS, HEADS * HD)
    keys = jnp.clip(jax.random.normal(jax.random.fold_in(key, 11), shape, jnp.float32), -6.0, 6.0)
    queries = jnp.clip(jax.random.normal(jax.random.fold_in(key, 12), shape, jnp.float32), -6.0, 6.0)
    return (queries, keys)


def draw_query(key, part):
    return drawn_pair(key)[0]


def draw_key(key, part):
    return drawn_pair(key)[1]


def shard_levels(key, dims, cuts, smallest, top_value):
    def one(position, parts):
        steps = jax.random.uniform(jax.random.fold_in(jax.random.fold_in(key, 6), position), (parts,), jnp.float32, smallest / len(cuts), top_value / len(cuts))
        return jnp.repeat(jnp.exp(steps), dims[position] // parts).reshape((-1,) + (1,) * (len(dims) - position - 1))

    loudness = one(*cuts[0])
    for cut in cuts[1:]:
        loudness = loudness * one(*cut)
    return loudness


def profile(amount, total, bound, slope):
    loads = [(1 << 20) // math.isqrt(grade ** slope) + 1 for grade in range(2, amount + 1)]
    surplus, given = total - bound - (amount - 1), [1] * (amount - 1)
    while surplus > 0:
        free = [i for i in range(amount - 1) if given[i] < bound]
        pool, remaining = sum([loads[i] for i in free]), surplus
        for i in free:
            addition = min(bound - given[i], max(1, remaining * loads[i] // pool), surplus)
            given[i] = given[i] + addition
            surplus = surplus - addition
    return np.array([bound] + given)


def uneven(key, number_of, total, limit, lean):
    if number_of == 2:
        one = jax.random.randint(key, (), max(1, total - limit), min(limit, total - 1) + 1)
        return jnp.stack([one, total - one])
    sizes = jnp.asarray(profile(number_of, total, limit, lean), jnp.int32)
    pairs = (number_of - 1) // 2
    giver, receiver = sizes[1:1 + 2 * pairs:2], sizes[2:2 + 2 * pairs:2]
    slack = jnp.minimum(giver - 1, limit - receiver)
    moved = jax.random.randint(jax.random.fold_in(key, 1), (pairs,), 0, 1 << 20) % (slack + 1)
    sizes = sizes.at[1:1 + 2 * pairs:2].set(giver - moved).at[2:2 + 2 * pairs:2].set(receiver + moved)
    return sizes[jax.random.permutation(jax.random.fold_in(key, 2), number_of)]


def normal_values(stream_key, dims, deviation, bound, shards=(), kind=jnp.bfloat16):
    drawn = deviation * jax.random.normal(stream_key, dims, jnp.float32)
    if shards:
        drawn = drawn * shard_levels(stream_key, dims, shards, -0.22, 0.18)
    return jnp.clip(drawn, -bound, bound).astype(kind)


def setup_inputs(seed: int = 0) -> dict:
    splits = jax.random.split(jax.random.key(seed), 11)
    return {
        "streams": normal_values(splits[0], (TOKENS, 3, CH), 1.0, 6.0, ((0, 32),), jnp.float32),
        "se_filter": normal_values(splits[1], (SE_LEN, 3, GROUPS), 0.45, 3.0, (), jnp.float32),
        "mr_filter": normal_values(splits[2], (MR_LEN, GROUPS), 0.25, 1.5, (), jnp.float32),
        "mr_decay": jnp.clip(jnp.exp(jax.random.uniform(splits[3], (GROUPS,), jnp.float32, math.log(0.004), math.log(0.1))), 0.004, 0.1),
        "query": draw_query(jax.random.fold_in(splits[10], 71), 0),
        "key": draw_key(jax.random.fold_in(splits[10], 71), 0),
        "value": normal_values(splits[6], (TOKENS, CH), 1.0, 6.0, ((0, 32),), jnp.float32),
        "placement_list": jax.random.permutation(splits[7], N_SEQ).astype(jnp.int32),
        "doc_ids": jnp.searchsorted(jnp.cumsum(uneven(splits[8], DOCS, TOKENS, TOKENS // 4, 2)), jnp.arange(TOKENS), side="right").astype(jnp.int32),
        "norm_gain": jnp.clip(1.0 + 0.15 * jax.random.normal(splits[9], (CH,), jnp.float32), 0.25, 1.75),
    }


def shifted(x, lag, fill):
    if lag == 0:
        return x
    front = jnp.full((lag,) + x.shape[1:], fill, x.dtype)
    return jnp.concatenate([front, x[:x.shape[0] - lag]], axis=0)

def reference(streams, se_filter, mr_filter, mr_decay, query, key, value, placement_list, doc_ids, norm_gain):
    inverse = jnp.zeros((N_SEQ,), jnp.int32).at[placement_list].set(jnp.arange(N_SEQ, dtype=jnp.int32))

    def natural(x):
        return x.reshape((N_SEQ, TOK_DEV) + x.shape[1:])[inverse].reshape(x.shape)

    def stored(x):
        return x.reshape((N_SEQ, TOK_DEV) + x.shape[1:])[placement_list].reshape(x.shape)
    seq_streams = natural(streams)
    seq_query = natural(query)
    seq_key = natural(key)
    seq_value = natural(value)
    docs = doc_ids.astype(jnp.int32)
    short_taps = jnp.repeat(se_filter, GROUP, axis=2)
    featured = jnp.zeros((TOKENS, 3, CH), jnp.float32)
    for lag in range(SE_LEN):
        same = (shifted(docs, lag, -1) == docs)[:, None, None]
        featured = featured + jnp.where(same, short_taps[lag][None] * shifted(seq_streams, lag, 0.0), 0.0)
    gated = featured[:, 1] * featured[:, 2]
    lags = jnp.arange(MR_LEN, dtype=jnp.float32)[:, None]
    taps = mr_filter * jnp.exp(-mr_decay[None, :] * lags)
    long_taps = jnp.repeat(taps, GROUP, axis=1)
    conv = jnp.zeros((TOKENS, CH), jnp.float32)
    for lag in range(MR_LEN):
        same = (shifted(docs, lag, -1) == docs)[:, None]
        conv = conv + jnp.where(same, long_taps[lag][None] * shifted(gated, lag, 0.0), 0.0)
    hyena = featured[:, 0] * conv
    positions = jnp.arange(TOKENS, dtype=jnp.int32)
    allowed = (positions[None, :] <= positions[:, None]) & (docs[None, :] == docs[:, None])
    heads_q = seq_query.reshape(TOKENS, HEADS, HD).transpose(1, 0, 2)
    heads_k = seq_key.reshape(TOKENS, HEADS, HD).transpose(1, 0, 2)
    heads_v = seq_value.reshape(TOKENS, HEADS, HD).transpose(1, 0, 2)

    def one_head(args):
        qq, kk, vv = args
        scores = jnp.dot(qq, kk.T, precision=lax.Precision.HIGHEST) / jnp.sqrt(jnp.float32(HD))
        scores = jnp.where(allowed, scores, jnp.float32(-1e+30))
        top = lax.optimization_barrier(jnp.max(scores, axis=1, keepdims=True))
        weights = jnp.where(allowed, jnp.exp(scores - top), 0.0)
        total = lax.optimization_barrier(jnp.sum(weights, axis=1, keepdims=True))
        return jnp.dot(weights, vv, precision=lax.Precision.HIGHEST) / total
    attended = lax.map(one_head, (heads_q, heads_k, heads_v)).transpose(1, 0, 2).reshape(TOKENS, CH)
    summed = hyena + attended
    scale = lax.rsqrt(lax.optimization_barrier(jnp.mean(summed * summed, axis=1, keepdims=True)) + 1e-05)
    return stored(summed * scale * norm_gain[None, :])
```

```python
import functools

import jax
import jax.numpy as jnp
from jax import lax
from jax.experimental import pallas as pl
from jax.experimental.pallas import tpu as pltpu
from jax.sharding import PartitionSpec as P

HD = 128
TILE = 256
NT = (((1,), (1,)), ((), ()))


def halves(x):
    high = x.astype(jnp.bfloat16)
    return high, (x - high.astype(jnp.float32)).astype(jnp.bfloat16)


def mul(a, b):
    return jnp.dot(a, b, preferred_element_type=jnp.float32)


def hyena_kernel(
    group_w, inv_ref, doc_ref, s_ref, short_ref, long_ref, docs_ref, place_ref, out_ref,
    ext, window, long_hi, long_lo,
):
    count, streams, tok, width = s_ref.shape
    lags = short_ref.shape[0]
    groups = width // group_w
    lead = ext.shape[1] - tok
    long_hi[...], long_lo[...] = halves(long_ref[...])
    ext[...] = jnp.zeros_like(ext)
    window[...] = jnp.zeros_like(window)
    lane_group = lax.broadcasted_iota(jnp.int32, (tok, width), 1) // group_w

    def stretch(c, carry):
        b = inv_ref[c]
        place = place_ref[pl.ds(pl.multiple_of(c * tok, tok), tok), :]
        for j in range(streams):
            ext[j, :lead] = ext[j, tok:]
            ext[j, lead:] = s_ref[b, j]
        featured = []
        for j in range(streams):
            total = short_ref[0, j][None, :] * ext[j, lead:]
            for lag in range(1, lags):
                term = short_ref[lag, j][None, :] * ext[j, lead - lag : lead - lag + tok]
                total = total + jnp.where(place >= lag, term, 0.0)
            featured.append(total)
        window[:tok] = window[tok:]
        window[tok:] = featured[1] * featured[2]
        docs = docs_ref[pl.ds(pl.multiple_of(c * tok, tok), 2 * tok), :]

        def document(d, conv):
            hi, lo = halves(jnp.where(docs == d, window[...], 0.0))
            both = mul(long_hi[...], jnp.concatenate([hi, lo], axis=1))
            full = both[:, :width] + both[:, width:] + mul(long_lo[...], hi)
            part = jnp.zeros((tok, width), jnp.float32)
            for g in range(groups):
                part = jnp.where(lane_group == g, full[g * tok : (g + 1) * tok], part)
            return jnp.where(docs[tok:] == d, part, conv)

        conv = lax.fori_loop(
            doc_ref[c * tok],
            doc_ref[c * tok + tok - 1] + 1,
            document,
            jnp.zeros((tok, width), jnp.float32),
        )
        out_ref[b] = featured[0] * conv
        return carry

    lax.fori_loop(0, count, stretch, 0)


def attention_kernel(
    scale, inv_ref, start_ref, x_ref, hyena_ref, starts_ref, out_ref, keys, values
):
    count, _, tok, width = x_ref.shape
    per = TILE // tok

    def prepare(c, carry):
        rows = pl.ds(pl.multiple_of(c * tok, tok), tok)
        b = inv_ref[c]
        keys[rows, :] = jnp.concatenate(halves(x_ref[b, 1]), axis=1)
        values[rows, :] = jnp.concatenate(halves(x_ref[b, 2]), axis=1)
        return carry

    lax.fori_loop(0, count, prepare, 0)

    def rows_of(i, carry):
        stored = [inv_ref[i * per + r] for r in range(per)]
        q = jnp.concatenate([x_ref[b, 0] for b in stored], axis=0) * scale
        q_hi, q_lo = halves(q)
        q_both = jnp.concatenate([q_hi, q_hi], axis=1)
        starts = starts_ref[pl.ds(pl.multiple_of(i * TILE, TILE), TILE), :]
        row = i * TILE + lax.broadcasted_iota(jnp.int32, (TILE, TILE), 0)
        lane = lax.broadcasted_iota(jnp.int32, (TILE, TILE), 1)

        def block(j, carry):
            top, total, acc = carry
            rows = pl.ds(pl.multiple_of(j * TILE, TILE), TILE)
            k = keys[rows, :]
            s = lax.dot_general(q_both, k, NT, preferred_element_type=jnp.float32)
            s = s + lax.dot_general(q_lo, k[:, :width], NT, preferred_element_type=jnp.float32)
            col = j * TILE + lane
            allowed = (col >= starts) & (col <= row)
            s = jnp.where(allowed, s, -1e30)
            new = jnp.maximum(top, jnp.max(s, axis=1, keepdims=True))
            w = jnp.where(allowed, jnp.exp(s - new), 0.0)
            fade = jnp.exp(top - new)
            w_hi, w_lo = halves(w)
            v = values[rows, :]
            both = mul(w_hi, v)
            got = both[:, :width] + both[:, width:] + mul(w_lo, v[:, :width])
            return new, fade * total + jnp.sum(w, axis=1, keepdims=True), fade * acc + got

        first = lax.div(start_ref[i * TILE], TILE)
        top, total, acc = lax.fori_loop(
            first,
            i + 1,
            block,
            (
                jnp.full((TILE, 1), -1e30, jnp.float32),
                jnp.zeros((TILE, 1), jnp.float32),
                jnp.zeros((TILE, width), jnp.float32),
            ),
        )
        attended = acc / total
        for r, b in enumerate(stored):
            out_ref[b] = attended[r * tok : (r + 1) * tok] + hyena_ref[b]
        return carry

    lax.fori_loop(0, count // per, rows_of, 0)


def split_heads(
    streams, se_filter, mr_filter, mr_decay, query, key, value, placement_list, doc_ids, norm_gain
):
    tok, kinds, chl = streams.shape
    se_len, _, groups_l = se_filter.shape
    mr_len = mr_filter.shape[0]
    count = placement_list.shape[0]
    group_w = chl // groups_l
    width = chl // count
    groups = groups_l // count
    tokens = count * tok
    me = lax.axis_index("seq")
    index = jnp.arange(count, dtype=jnp.int32)
    inverse = jnp.sum(
        jnp.where(placement_list[None, :] == index[:, None], index[None, :], 0), axis=1
    )
    positions = jnp.arange(tokens, dtype=jnp.int32)
    fresh = jnp.concatenate([jnp.ones((1,), bool), doc_ids[1:] != doc_ids[:-1]])
    starts = lax.cummax(jnp.where(fresh, positions, 0))
    docs = jnp.concatenate([jnp.full((tok,), -1, jnp.int32), doc_ids])

    def exchange(x):
        return lax.all_to_all(x, "seq", 0, 0, tiled=True)

    with jax.named_scope("streams_to_channels"):
        sent = streams.reshape(tok, kinds, count, width).transpose(2, 1, 0, 3)
        by_channel = exchange(sent)
    with jax.named_scope("qkv_to_heads"):
        stacked = jnp.stack([query, key, value], axis=0).reshape(3, tok, count, width)
        by_head = exchange(stacked.transpose(2, 0, 1, 3))

    with jax.named_scope("filters"):
        short = lax.dynamic_slice_in_dim(se_filter, me * groups, groups, 2)
        short = jnp.repeat(short, group_w, axis=2)
        decays = jnp.arange(mr_len, dtype=jnp.float32)[:, None]
        taps = lax.dynamic_slice_in_dim(mr_filter, me * groups, groups, 1)
        decay = lax.dynamic_slice_in_dim(mr_decay, me * groups, groups, 0)
        taps = (taps * jnp.exp(-decay[None, :] * decays)).T
        period = 3 * tok
        line = jnp.concatenate(
            [
                jnp.zeros((groups, tok - mr_len + 1), jnp.float32),
                taps[:, ::-1],
                jnp.zeros((groups, period - tok - 1), jnp.float32),
            ],
            axis=1,
        )
        sheared = jnp.tile(line, (1, tok))[:, : tok * (period - 1)]
        long = sheared.reshape(groups, tok, period - 1)[:, :, : 2 * tok]
        long = long.reshape(groups * tok, 2 * tok)

    smem = pl.BlockSpec(memory_space=pltpu.SMEM)
    vmem = pl.BlockSpec(memory_space=pltpu.VMEM)
    shape = jax.ShapeDtypeStruct((count, tok, width), jnp.float32)
    params = pltpu.CompilerParams(vmem_limit_bytes=56 * 2**20)
    hyena = pl.pallas_call(
        functools.partial(hyena_kernel, group_w),
        out_shape=shape,
        in_specs=[smem, smem, vmem, vmem, vmem, vmem, vmem],
        out_specs=vmem,
        scratch_shapes=[
            pltpu.VMEM((kinds, tok + 8, width), jnp.float32),
            pltpu.VMEM((2 * tok, width), jnp.float32),
            pltpu.VMEM((groups * tok, 2 * tok), jnp.bfloat16),
            pltpu.VMEM((groups * tok, 2 * tok), jnp.bfloat16),
        ],
        compiler_params=params,
        cost_estimate=pl.CostEstimate(
            flops=40 * 6 * groups * tok * 2 * tok * width, bytes_accessed=12 * 2**20,
            transcendentals=0,
        ),
        name="hyena",
    )(
        inverse, doc_ids, by_channel, short, long, docs[:, None], (positions - starts)[:, None]
    )
    summed = pl.pallas_call(
        functools.partial(attention_kernel, 1.0 / HD**0.5),
        out_shape=shape,
        in_specs=[smem, smem, vmem, vmem, vmem],
        out_specs=vmem,
        scratch_shapes=[
            pltpu.VMEM((tokens, 2 * width), jnp.bfloat16),
            pltpu.VMEM((tokens, 2 * width), jnp.bfloat16),
        ],
        compiler_params=params,
        cost_estimate=pl.CostEstimate(
            flops=12 * tokens * 1024 * width, bytes_accessed=12 * 2**20,
            transcendentals=tokens * 1024,
        ),
        name="attention",
    )(inverse, starts, by_head, hyena, starts[:, None])
    with jax.named_scope("back_to_tokens"):
        back = exchange(summed)
        summed = back.transpose(1, 0, 2).reshape(tok, chl)
    row_squares = lax.psum(jnp.sum(summed * summed, axis=1), "mp")
    norm_scale = lax.rsqrt(row_squares / (chl * lax.axis_size("mp")) + 1e-05)
    return summed * norm_scale[:, None] * norm_gain[None, :]


def fits(tok, chl, groups_l, se_len, mr_len, count):
    return (
        chl == count * HD
        and groups_l % count == 0
        and TILE % tok == 0
        and tok >= 128
        and (count * tok) % TILE == 0
        and mr_len <= tok
        and se_len <= 9
    )


def per_device(*args):
    streams, se_filter, mr_filter = args[:3]
    sizes = (streams.shape[0], streams.shape[2], se_filter.shape[2])
    if fits(*sizes, se_filter.shape[0], mr_filter.shape[0], args[7].shape[0]):
        return split_heads(*args)
    return gather_all(*args)


def gather_all(
    streams, se_filter, mr_filter, mr_decay, query, key, value, placement_list, doc_ids, norm_gain
):
    tok = streams.shape[0]
    chl = streams.shape[2]
    groups_l = se_filter.shape[2]
    group_w = chl // groups_l
    se_len = se_filter.shape[0]
    mr_len = mr_filter.shape[0]
    heads_l = chl // HD
    seq_count = placement_list.shape[0]
    device = lax.axis_index("seq")
    stretch = placement_list[device]
    listing = jnp.arange(seq_count, dtype=jnp.int32)
    source = jnp.sum(jnp.where(placement_list == stretch - 1, listing, 0))
    base = stretch * tok
    offsets = jnp.arange(tok, dtype=jnp.int32)
    local_pos = base + offsets
    local_doc = lax.dynamic_slice_in_dim(doc_ids, base, tok)

    def earlier_docs(width):
        where_pos = base - width + jnp.arange(width, dtype=jnp.int32)
        found = doc_ids[jnp.clip(where_pos, 0, doc_ids.shape[0] - 1)]
        return jnp.where(where_pos >= 0, found, -1)

    def pick(piece):
        owner = jnp.arange(piece.shape[0], dtype=jnp.int32) == source
        mask = owner.reshape((piece.shape[0],) + (1,) * (piece.ndim - 1))
        return jnp.sum(jnp.where(mask, piece, 0.0), axis=0)

    short_tail = pick(
        lax.all_gather(streams[tok - (se_len - 1) :][None], "seq", axis=0, tiled=True)
    )
    extended = jnp.concatenate([short_tail, streams], axis=0)
    ext_doc = jnp.concatenate([earlier_docs(se_len - 1), local_doc])
    short_taps = jnp.repeat(se_filter, group_w, axis=2)
    featured = jnp.zeros((tok, 3, chl), jnp.float32)
    for lag in range(se_len):
        first = se_len - 1 - lag
        same = (ext_doc[first : first + tok] == local_doc)[:, None, None]
        featured = featured + jnp.where(
            same, short_taps[lag][None] * extended[first : first + tok], 0.0
        )
    gated = featured[:, 1] * featured[:, 2]
    decays = jnp.arange(mr_len, dtype=jnp.float32)[:, None]
    taps = mr_filter * jnp.exp(-mr_decay[None, :] * decays)
    scale = 1.0 / jnp.sqrt(jnp.float32(HD))
    tail_piece = gated[tok - (mr_len - 1) :][None]
    long_tail = pick(lax.all_gather(tail_piece, "seq", axis=0, tiled=True))
    q_heads = query.reshape(tok, heads_l, HD)
    key_pos = (placement_list[:, None] * tok + offsets[None, :]).reshape(-1)
    key_doc = doc_ids[jnp.clip(key_pos, 0, doc_ids.shape[0] - 1)]
    allowed = (
        (key_pos >= 0)[None, :]
        & (key_pos[None, :] <= local_pos[:, None])
        & (key_doc[None, :] == local_doc[:, None])
    )[None]
    k_heads = lax.all_gather(key[None], "seq", axis=0, tiled=True).reshape(-1, heads_l, HD)
    v_heads = lax.all_gather(value[None], "seq", axis=0, tiled=True).reshape(-1, heads_l, HD)
    top_old = jnp.full((heads_l, tok), -1e30, jnp.float32)
    scores = jnp.einsum("qhd,khd->hqk", q_heads, k_heads, precision=lax.Precision.HIGHEST) * scale
    scores = jnp.where(allowed, scores, jnp.float32(-1e30))
    top_new = jnp.maximum(top_old, jnp.max(scores, axis=2))
    weights = jnp.where(allowed, jnp.exp(scores - top_new[:, :, None]), 0.0)
    total_new = jnp.sum(weights, axis=2)
    acc_new = jnp.einsum("hqk,khd->hqd", weights, v_heads, precision=lax.Precision.HIGHEST)
    attended = (acc_new / total_new[:, :, None]).transpose(1, 0, 2).reshape(tok, chl)
    span = tok + mr_len - 1
    ext_rows = jnp.concatenate([long_tail, gated], axis=0)
    doc_rows = jnp.concatenate([earlier_docs(mr_len - 1), local_doc])
    lag = (
        jnp.arange(tok, dtype=jnp.int32)[:, None]
        + (mr_len - 1)
        - jnp.arange(span, dtype=jnp.int32)[None, :]
    )
    valid = (lag >= 0) & (lag < mr_len) & (doc_rows[None, :] == local_doc[:, None])
    toeplitz = jnp.where(valid[:, :, None], taps[jnp.clip(lag, 0, mr_len - 1)], 0.0)
    conv = jnp.einsum(
        "tsg,sgc->tgc",
        toeplitz,
        ext_rows.reshape(span, groups_l, group_w),
        precision=lax.Precision.HIGHEST,
    ).reshape(tok, chl)
    hyena = featured[:, 0] * conv
    summed = hyena + attended
    row_squares = lax.psum(jnp.sum(summed * summed, axis=1), "mp")
    norm_scale = lax.rsqrt(row_squares / (chl * lax.axis_size("mp")) + 1e-05)
    return summed * norm_scale[:, None] * norm_gain[None, :]


def solution(mesh):
    placed = (
        P("seq", None, "mp"),
        P(None, None, "mp"),
        P(None, "mp"),
        P("mp"),
        P("seq", "mp"),
        P("seq", "mp"),
        P("seq", "mp"),
        P(),
        P(),
        P("mp"),
    )
    return jax.shard_map(
        per_device, mesh=mesh, in_specs=placed, out_specs=P("seq", "mp"), check_vma=False
    )
```

```python
import functools

import jax
import jax.numpy as jnp
from jax import lax
from jax.experimental import pallas as pl
from jax.experimental.pallas import tpu as pltpu
from jax.sharding import PartitionSpec as P

HD = 128
TILE = 256
NT = (((1,), (1,)), ((), ()))


def halves(x):
    high = x.astype(jnp.bfloat16)
    return high, (x - high.astype(jnp.float32)).astype(jnp.bfloat16)


def mul(a, b):
    return jnp.dot(a, b, preferred_element_type=jnp.float32)


def conv_kernel(
    group_w, inv_ref, doc_ref, gated_ref, long_ref, docs_ref, out_ref, window, long_hi, long_lo
):
    count, tok, width = gated_ref.shape
    groups = width // group_w
    long_hi[...], long_lo[...] = halves(long_ref[...])
    window[...] = jnp.zeros_like(window)
    lane_group = lax.broadcasted_iota(jnp.int32, (tok, width), 1) // group_w

    def stretch(c, carry):
        b = inv_ref[c]
        window[:tok] = window[tok:]
        window[tok:] = gated_ref[b]
        docs = docs_ref[pl.ds(pl.multiple_of(c * tok, tok), 2 * tok), :]

        def document(d, conv):
            hi, lo = halves(jnp.where(docs == d, window[...], 0.0))
            both = mul(long_hi[...], jnp.concatenate([hi, lo], axis=1))
            full = both[:, :width] + both[:, width:] + mul(long_lo[...], hi)
            part = jnp.zeros((tok, width), jnp.float32)
            for g in range(groups):
                part = jnp.where(lane_group == g, full[g * tok : (g + 1) * tok], part)
            return jnp.where(docs[tok:] == d, part, conv)

        out_ref[b] = lax.fori_loop(
            doc_ref[c * tok],
            doc_ref[c * tok + tok - 1] + 1,
            document,
            jnp.zeros((tok, width), jnp.float32),
        )
        return carry

    lax.fori_loop(0, count, stretch, 0)


def attention_kernel(
    scale, inv_ref, start_ref, x_ref, starts_ref, out_ref, keys, values
):
    count, _, tok, width = x_ref.shape
    per = TILE // tok

    def prepare(c, carry):
        rows = pl.ds(pl.multiple_of(c * tok, tok), tok)
        b = inv_ref[c]
        keys[rows, :] = jnp.concatenate(halves(x_ref[b, 1]), axis=1)
        values[rows, :] = jnp.concatenate(halves(x_ref[b, 2]), axis=1)
        return carry

    lax.fori_loop(0, count, prepare, 0)

    def rows_of(i, carry):
        stored = [inv_ref[i * per + r] for r in range(per)]
        q = jnp.concatenate([x_ref[b, 0] for b in stored], axis=0) * scale
        q_hi, q_lo = halves(q)
        q_both = jnp.concatenate([q_hi, q_hi], axis=1)
        starts = starts_ref[pl.ds(pl.multiple_of(i * TILE, TILE), TILE), :]
        row = i * TILE + lax.broadcasted_iota(jnp.int32, (TILE, TILE), 0)
        lane = lax.broadcasted_iota(jnp.int32, (TILE, TILE), 1)

        def block(j, carry):
            top, total, acc = carry
            rows = pl.ds(pl.multiple_of(j * TILE, TILE), TILE)
            k = keys[rows, :]
            s = lax.dot_general(q_both, k, NT, preferred_element_type=jnp.float32)
            s = s + lax.dot_general(q_lo, k[:, :width], NT, preferred_element_type=jnp.float32)
            col = j * TILE + lane
            allowed = (col >= starts) & (col <= row)
            s = jnp.where(allowed, s, -1e30)
            new = jnp.maximum(top, jnp.max(s, axis=1, keepdims=True))
            w = jnp.where(allowed, jnp.exp(s - new), 0.0)
            fade = jnp.exp(top - new)
            w_hi, w_lo = halves(w)
            v = values[rows, :]
            both = mul(w_hi, v)
            got = both[:, :width] + both[:, width:] + mul(w_lo, v[:, :width])
            return new, fade * total + jnp.sum(w, axis=1, keepdims=True), fade * acc + got

        first = lax.div(start_ref[i * TILE], TILE)
        top, total, acc = lax.fori_loop(
            first,
            i + 1,
            block,
            (
                jnp.full((TILE, 1), -1e30, jnp.float32),
                jnp.zeros((TILE, 1), jnp.float32),
                jnp.zeros((TILE, width), jnp.float32),
            ),
        )
        attended = acc / total
        for r, b in enumerate(stored):
            out_ref[b] = attended[r * tok : (r + 1) * tok]
        return carry

    lax.fori_loop(0, count // per, rows_of, 0)


def split_heads(
    streams, se_filter, mr_filter, mr_decay, query, key, value, placement_list, doc_ids, norm_gain
):
    tok, kinds, chl = streams.shape
    se_len, _, groups_l = se_filter.shape
    mr_len = mr_filter.shape[0]
    count = placement_list.shape[0]
    group_w = chl // groups_l
    width = chl // count
    groups = groups_l // count
    tokens = count * tok
    me = lax.axis_index("seq")
    index = jnp.arange(count, dtype=jnp.int32)
    inverse = jnp.sum(
        jnp.where(placement_list[None, :] == index[:, None], index[None, :], 0), axis=1
    )
    positions = jnp.arange(tokens, dtype=jnp.int32)
    fresh = jnp.concatenate([jnp.ones((1,), bool), doc_ids[1:] != doc_ids[:-1]])
    starts = lax.cummax(jnp.where(fresh, positions, 0))
    docs = jnp.concatenate([jnp.full((tok,), -1, jnp.int32), doc_ids])

    def exchange(x):
        return lax.all_to_all(x, "seq", 0, 0, tiled=True)

    def to_tokens(x):
        return exchange(x).transpose(1, 0, 2).reshape(-1, chl)

    reach = se_len - 1
    stretch = placement_list[me]
    with jax.named_scope("tails_to_next_stretch"):
        tails = streams[tok - reach :].reshape(reach * kinds, count, width)
        tails = exchange(tails.transpose(1, 0, 2))
        before = placement_list[:, None] - 1 == placement_list[None, :]
        source = jnp.sum(jnp.where(before, index[None, :], 0), axis=1)
        tail = to_tokens(tails[source]).reshape(reach, kinds, chl)
    with jax.named_scope("qkv_to_heads"):
        stacked = jnp.stack([query, key, value], axis=0).reshape(3, tok, count, width)
        stacked, tail = lax.optimization_barrier((stacked.transpose(2, 0, 1, 3), tail))
        by_head = exchange(stacked)
    with jax.named_scope("featured"):
        place = lax.dynamic_slice_in_dim(positions - starts, stretch * tok, tok)
        extended = jnp.concatenate([tail, streams], axis=0)
        short = jnp.repeat(se_filter, group_w, axis=2)
        featured = short[0][None] * streams
        for lag in range(1, se_len):
            term = short[lag][None] * extended[reach - lag : reach - lag + tok]
            featured = featured + jnp.where((place >= lag)[:, None, None], term, 0.0)
        gated = featured[:, 1] * featured[:, 2]
    with jax.named_scope("gated_to_channels"):
        by_channel = exchange(gated.reshape(tok, count, width).transpose(1, 0, 2))

    with jax.named_scope("filters"):
        decays = jnp.arange(mr_len, dtype=jnp.float32)[:, None]
        taps = lax.dynamic_slice_in_dim(mr_filter, me * groups, groups, 1)
        decay = lax.dynamic_slice_in_dim(mr_decay, me * groups, groups, 0)
        taps = (taps * jnp.exp(-decay[None, :] * decays)).T
        period = 3 * tok
        line = jnp.concatenate(
            [
                jnp.zeros((groups, tok - mr_len + 1), jnp.float32),
                taps[:, ::-1],
                jnp.zeros((groups, period - tok - 1), jnp.float32),
            ],
            axis=1,
        )
        sheared = jnp.tile(line, (1, tok))[:, : tok * (period - 1)]
        long = sheared.reshape(groups, tok, period - 1)[:, :, : 2 * tok]
        long = long.reshape(groups * tok, 2 * tok)

    smem = pl.BlockSpec(memory_space=pltpu.SMEM)
    vmem = pl.BlockSpec(memory_space=pltpu.VMEM)
    shape = jax.ShapeDtypeStruct((count, tok, width), jnp.float32)
    params = pltpu.CompilerParams(vmem_limit_bytes=56 * 2**20)
    attended = pl.pallas_call(
        functools.partial(attention_kernel, 1.0 / HD**0.5),
        out_shape=shape,
        in_specs=[smem, smem, vmem, vmem],
        out_specs=vmem,
        scratch_shapes=[
            pltpu.VMEM((tokens, 2 * width), jnp.bfloat16),
            pltpu.VMEM((tokens, 2 * width), jnp.bfloat16),
        ],
        compiler_params=params,
        cost_estimate=pl.CostEstimate(
            flops=40 * tokens * 1024 * width, bytes_accessed=12 * 2**20,
            transcendentals=tokens * 1024,
        ),
        name="attention",
    )(inverse, starts, by_head, starts[:, None])
    conv = pl.pallas_call(
        functools.partial(conv_kernel, group_w),
        out_shape=shape,
        in_specs=[smem, smem, vmem, vmem, vmem],
        out_specs=vmem,
        scratch_shapes=[
            pltpu.VMEM((2 * tok, width), jnp.float32),
            pltpu.VMEM((groups * tok, 2 * tok), jnp.bfloat16),
            pltpu.VMEM((groups * tok, 2 * tok), jnp.bfloat16),
        ],
        compiler_params=params,
        cost_estimate=pl.CostEstimate(
            flops=40 * 8 * groups * tok * 2 * tok * width, bytes_accessed=12 * 2**20,
            transcendentals=0,
        ),
        name="conv",
    )(inverse, doc_ids, by_channel, long, docs[:, None])
    with jax.named_scope("back_to_tokens"):
        attended = to_tokens(attended)
        summed = featured[:, 0] * to_tokens(conv) + attended
    row_squares = lax.psum(jnp.sum(summed * summed, axis=1), "mp")
    norm_scale = lax.rsqrt(row_squares / (chl * lax.axis_size("mp")) + 1e-05)
    return summed * norm_scale[:, None] * norm_gain[None, :]


def fits(tok, chl, groups_l, se_len, mr_len, count):
    return (
        chl == count * HD
        and groups_l % count == 0
        and TILE % tok == 0
        and tok >= 128
        and (count * tok) % TILE == 0
        and mr_len <= tok
        and se_len <= 9
    )


def per_device(*args):
    streams, se_filter, mr_filter = args[:3]
    sizes = (streams.shape[0], streams.shape[2], se_filter.shape[2])
    if fits(*sizes, se_filter.shape[0], mr_filter.shape[0], args[7].shape[0]):
        return split_heads(*args)
    return gather_all(*args)


def gather_all(
    streams, se_filter, mr_filter, mr_decay, query, key, value, placement_list, doc_ids, norm_gain
):
    tok = streams.shape[0]
    chl = streams.shape[2]
    groups_l = se_filter.shape[2]
    group_w = chl // groups_l
    se_len = se_filter.shape[0]
    mr_len = mr_filter.shape[0]
    heads_l = chl // HD
    seq_count = placement_list.shape[0]
    device = lax.axis_index("seq")
    stretch = placement_list[device]
    listing = jnp.arange(seq_count, dtype=jnp.int32)
    source = jnp.sum(jnp.where(placement_list == stretch - 1, listing, 0))
    base = stretch * tok
    offsets = jnp.arange(tok, dtype=jnp.int32)
    local_pos = base + offsets
    local_doc = lax.dynamic_slice_in_dim(doc_ids, base, tok)

    def earlier_docs(width):
        where_pos = base - width + jnp.arange(width, dtype=jnp.int32)
        found = doc_ids[jnp.clip(where_pos, 0, doc_ids.shape[0] - 1)]
        return jnp.where(where_pos >= 0, found, -1)

    def pick(piece):
        owner = jnp.arange(piece.shape[0], dtype=jnp.int32) == source
        mask = owner.reshape((piece.shape[0],) + (1,) * (piece.ndim - 1))
        return jnp.sum(jnp.where(mask, piece, 0.0), axis=0)

    short_tail = pick(
        lax.all_gather(streams[tok - (se_len - 1) :][None], "seq", axis=0, tiled=True)
    )
    extended = jnp.concatenate([short_tail, streams], axis=0)
    ext_doc = jnp.concatenate([earlier_docs(se_len - 1), local_doc])
    short_taps = jnp.repeat(se_filter, group_w, axis=2)
    featured = jnp.zeros((tok, 3, chl), jnp.float32)
    for lag in range(se_len):
        first = se_len - 1 - lag
        same = (ext_doc[first : first + tok] == local_doc)[:, None, None]
        featured = featured + jnp.where(
            same, short_taps[lag][None] * extended[first : first + tok], 0.0
        )
    gated = featured[:, 1] * featured[:, 2]
    decays = jnp.arange(mr_len, dtype=jnp.float32)[:, None]
    taps = mr_filter * jnp.exp(-mr_decay[None, :] * decays)
    scale = 1.0 / jnp.sqrt(jnp.float32(HD))
    tail_piece = gated[tok - (mr_len - 1) :][None]
    long_tail = pick(lax.all_gather(tail_piece, "seq", axis=0, tiled=True))
    q_heads = query.reshape(tok, heads_l, HD)
    key_pos = (placement_list[:, None] * tok + offsets[None, :]).reshape(-1)
    key_doc = doc_ids[jnp.clip(key_pos, 0, doc_ids.shape[0] - 1)]
    allowed = (
        (key_pos >= 0)[None, :]
        & (key_pos[None, :] <= local_pos[:, None])
        & (key_doc[None, :] == local_doc[:, None])
    )[None]
    k_heads = lax.all_gather(key[None], "seq", axis=0, tiled=True).reshape(-1, heads_l, HD)
    v_heads = lax.all_gather(value[None], "seq", axis=0, tiled=True).reshape(-1, heads_l, HD)
    top_old = jnp.full((heads_l, tok), -1e30, jnp.float32)
    scores = jnp.einsum("qhd,khd->hqk", q_heads, k_heads, precision=lax.Precision.HIGHEST) * scale
    scores = jnp.where(allowed, scores, jnp.float32(-1e30))
    top_new = jnp.maximum(top_old, jnp.max(scores, axis=2))
    weights = jnp.where(allowed, jnp.exp(scores - top_new[:, :, None]), 0.0)
    total_new = jnp.sum(weights, axis=2)
    acc_new = jnp.einsum("hqk,khd->hqd", weights, v_heads, precision=lax.Precision.HIGHEST)
    attended = (acc_new / total_new[:, :, None]).transpose(1, 0, 2).reshape(tok, chl)
    span = tok + mr_len - 1
    ext_rows = jnp.concatenate([long_tail, gated], axis=0)
    doc_rows = jnp.concatenate([earlier_docs(mr_len - 1), local_doc])
    lag = (
        jnp.arange(tok, dtype=jnp.int32)[:, None]
        + (mr_len - 1)
        - jnp.arange(span, dtype=jnp.int32)[None, :]
    )
    valid = (lag >= 0) & (lag < mr_len) & (doc_rows[None, :] == local_doc[:, None])
    toeplitz = jnp.where(valid[:, :, None], taps[jnp.clip(lag, 0, mr_len - 1)], 0.0)
    conv = jnp.einsum(
        "tsg,sgc->tgc",
        toeplitz,
        ext_rows.reshape(span, groups_l, group_w),
        precision=lax.Precision.HIGHEST,
    ).reshape(tok, chl)
    hyena = featured[:, 0] * conv
    summed = hyena + attended
    row_squares = lax.psum(jnp.sum(summed * summed, axis=1), "mp")
    norm_scale = lax.rsqrt(row_squares / (chl * lax.axis_size("mp")) + 1e-05)
    return summed * norm_scale[:, None] * norm_gain[None, :]


def solution(mesh):
    placed = (
        P("seq", None, "mp"),
        P(None, None, "mp"),
        P(None, "mp"),
        P("mp"),
        P("seq", "mp"),
        P("seq", "mp"),
        P("seq", "mp"),
        P(),
        P(),
        P("mp"),
    )
    return jax.shard_map(
        per_device, mesh=mesh, in_specs=placed, out_specs=P("seq", "mp"), check_vma=False
    )
```

```python
import functools

import jax
import jax.numpy as jnp
from jax import lax
from jax.experimental import pallas as pl
from jax.experimental.pallas import tpu as pltpu
from jax.sharding import PartitionSpec as P

HD = 128
TILE = 256
NT = (((1,), (1,)), ((), ()))


def halves(x):
    high = x.astype(jnp.bfloat16)
    return high, (x - high.astype(jnp.float32)).astype(jnp.bfloat16)


def mul(a, b):
    return jnp.dot(a, b, preferred_element_type=jnp.float32)


def conv_kernel(
    group_w, inv_ref, doc_ref, gated_ref, long_ref, docs_ref, out_ref, window, long_hi, long_lo
):
    count, tok, width = gated_ref.shape
    groups = width // group_w
    long_hi[...], long_lo[...] = halves(long_ref[...])
    window[...] = jnp.zeros_like(window)
    lane_group = lax.broadcasted_iota(jnp.int32, (tok, width), 1) // group_w

    def stretch(c, carry):
        b = inv_ref[c]
        window[:tok] = window[tok:]
        window[tok:] = gated_ref[b]
        docs = docs_ref[pl.ds(pl.multiple_of(c * tok, tok), 2 * tok), :]

        def document(d, conv):
            hi, lo = halves(jnp.where(docs == d, window[...], 0.0))
            both = mul(long_hi[...], jnp.concatenate([hi, lo], axis=1))
            full = both[:, :width] + both[:, width:] + mul(long_lo[...], hi)
            part = jnp.zeros((tok, width), jnp.float32)
            for g in range(groups):
                part = jnp.where(lane_group == g, full[g * tok : (g + 1) * tok], part)
            return jnp.where(docs[tok:] == d, part, conv)

        out_ref[b] = lax.fori_loop(
            doc_ref[c * tok],
            doc_ref[c * tok + tok - 1] + 1,
            document,
            jnp.zeros((tok, width), jnp.float32),
        )
        return carry

    lax.fori_loop(0, count, stretch, 0)


def attention_kernel(
    scale, inv_ref, start_ref, q_ref, kv_ref, starts_ref, out_ref, keys, values
):
    count, tok, width = q_ref.shape
    per = TILE // tok

    def prepare(c, carry):
        rows = pl.ds(pl.multiple_of(c * tok, tok), tok)
        b = inv_ref[c]
        keys[rows, :] = jnp.concatenate(halves(kv_ref[b, 0]), axis=1)
        values[rows, :] = jnp.concatenate(halves(kv_ref[b, 1]), axis=1)
        return carry

    lax.fori_loop(0, count, prepare, 0)

    def rows_of(i, carry):
        stored = [inv_ref[i * per + r] for r in range(per)]
        q = jnp.concatenate([q_ref[b] for b in stored], axis=0) * scale
        q_hi, q_lo = halves(q)
        q_both = jnp.concatenate([q_hi, q_hi], axis=1)
        starts = starts_ref[pl.ds(pl.multiple_of(i * TILE, TILE), TILE), :]
        row = i * TILE + lax.broadcasted_iota(jnp.int32, (TILE, TILE), 0)
        lane = lax.broadcasted_iota(jnp.int32, (TILE, TILE), 1)

        def block(j, carry):
            top, total, acc = carry
            rows = pl.ds(pl.multiple_of(j * TILE, TILE), TILE)
            k = keys[rows, :]
            s = lax.dot_general(q_both, k, NT, preferred_element_type=jnp.float32)
            s = s + lax.dot_general(q_lo, k[:, :width], NT, preferred_element_type=jnp.float32)
            col = j * TILE + lane
            allowed = (col >= starts) & (col <= row)
            s = jnp.where(allowed, s, -1e30)
            new = jnp.maximum(top, jnp.max(s, axis=1, keepdims=True))
            w = jnp.where(allowed, jnp.exp(s - new), 0.0)
            fade = jnp.exp(top - new)
            w_hi, w_lo = halves(w)
            v = values[rows, :]
            both = mul(w_hi, v)
            got = both[:, :width] + both[:, width:] + mul(w_lo, v[:, :width])
            return new, fade * total + jnp.sum(w, axis=1, keepdims=True), fade * acc + got

        first = lax.div(start_ref[i * TILE], TILE)
        top, total, acc = lax.fori_loop(
            first,
            i + 1,
            block,
            (
                jnp.full((TILE, 1), -1e30, jnp.float32),
                jnp.zeros((TILE, 1), jnp.float32),
                jnp.zeros((TILE, width), jnp.float32),
            ),
        )
        attended = acc / total
        for r, b in enumerate(stored):
            out_ref[b] = attended[r * tok : (r + 1) * tok]
        return carry

    lax.fori_loop(0, count // per, rows_of, 0)


def split_heads(
    streams, se_filter, mr_filter, mr_decay, query, key, value, placement_list, doc_ids, norm_gain
):
    tok, kinds, chl = streams.shape
    se_len, _, groups_l = se_filter.shape
    mr_len = mr_filter.shape[0]
    count = placement_list.shape[0]
    group_w = chl // groups_l
    width = chl // count
    groups = groups_l // count
    tokens = count * tok
    me = lax.axis_index("seq")
    index = jnp.arange(count, dtype=jnp.int32)
    inverse = jnp.sum(
        jnp.where(placement_list[None, :] == index[:, None], index[None, :], 0), axis=1
    )
    positions = jnp.arange(tokens, dtype=jnp.int32)
    fresh = jnp.concatenate([jnp.ones((1,), bool), doc_ids[1:] != doc_ids[:-1]])
    starts = lax.cummax(jnp.where(fresh, positions, 0))
    docs = jnp.concatenate([jnp.full((tok,), -1, jnp.int32), doc_ids])

    def exchange(x):
        return lax.all_to_all(x, "seq", 0, 0, tiled=True)

    def as_tokens(x):
        return x.transpose(1, 0, 2).reshape(-1, chl)

    reach = se_len - 1
    stretch = placement_list[me]
    with jax.named_scope("tails_to_next_stretch"):
        tails = streams[tok - reach :].reshape(reach * kinds, count, width)
        tails = exchange(tails.transpose(1, 0, 2))
        before = placement_list[:, None] - 1 == placement_list[None, :]
        source = jnp.sum(jnp.where(before, index[None, :], 0), axis=1)
        tail = as_tokens(exchange(tails[source])).reshape(reach, kinds, chl)
    def by_block(x):
        return x.reshape(tok, count, width).transpose(1, 0, 2)

    with jax.named_scope("query_to_heads"):
        sent, tail = lax.optimization_barrier((by_block(query), tail))
        q_head = exchange(sent)
    with jax.named_scope("key_value_to_heads"):
        sent = jnp.stack([by_block(key), by_block(value)], axis=1)
        sent, q_head, tail = lax.optimization_barrier((sent, q_head, tail))
        kv_head = exchange(sent)
    with jax.named_scope("featured"):
        place = lax.dynamic_slice_in_dim(positions - starts, stretch * tok, tok)
        extended = jnp.concatenate([tail, streams], axis=0)
        short = jnp.repeat(se_filter, group_w, axis=2)
        featured = short[0][None] * streams
        for lag in range(1, se_len):
            term = short[lag][None] * extended[reach - lag : reach - lag + tok]
            featured = featured + jnp.where((place >= lag)[:, None, None], term, 0.0)
        gated = featured[:, 1] * featured[:, 2]
    with jax.named_scope("gated_to_channels"):
        sent, kv_head = lax.optimization_barrier((by_block(gated), kv_head))
        by_channel = exchange(sent)

    with jax.named_scope("filters"):
        decays = jnp.arange(mr_len, dtype=jnp.float32)[:, None]
        taps = lax.dynamic_slice_in_dim(mr_filter, me * groups, groups, 1)
        decay = lax.dynamic_slice_in_dim(mr_decay, me * groups, groups, 0)
        taps = (taps * jnp.exp(-decay[None, :] * decays)).T
        period = 3 * tok
        line = jnp.concatenate(
            [
                jnp.zeros((groups, tok - mr_len + 1), jnp.float32),
                taps[:, ::-1],
                jnp.zeros((groups, period - tok - 1), jnp.float32),
            ],
            axis=1,
        )
        sheared = jnp.tile(line, (1, tok))[:, : tok * (period - 1)]
        long = sheared.reshape(groups, tok, period - 1)[:, :, : 2 * tok]
        long = long.reshape(groups * tok, 2 * tok)

    smem = pl.BlockSpec(memory_space=pltpu.SMEM)
    vmem = pl.BlockSpec(memory_space=pltpu.VMEM)
    shape = jax.ShapeDtypeStruct((count, tok, width), jnp.float32)
    params = pltpu.CompilerParams(vmem_limit_bytes=56 * 2**20)
    attended = pl.pallas_call(
        functools.partial(attention_kernel, 1.0 / HD**0.5),
        out_shape=shape,
        in_specs=[smem, smem, vmem, vmem, vmem],
        out_specs=vmem,
        scratch_shapes=[
            pltpu.VMEM((tokens, 2 * width), jnp.bfloat16),
            pltpu.VMEM((tokens, 2 * width), jnp.bfloat16),
        ],
        compiler_params=params,
        cost_estimate=pl.CostEstimate(
            flops=40 * tokens * 1024 * width, bytes_accessed=12 * 2**20,
            transcendentals=tokens * 1024,
        ),
        name="attention",
    )(inverse, starts, q_head, kv_head, starts[:, None])
    by_channel, attended = lax.optimization_barrier((by_channel, attended))
    conv = pl.pallas_call(
        functools.partial(conv_kernel, group_w),
        out_shape=shape,
        in_specs=[smem, smem, vmem, vmem, vmem],
        out_specs=vmem,
        scratch_shapes=[
            pltpu.VMEM((2 * tok, width), jnp.float32),
            pltpu.VMEM((groups * tok, 2 * tok), jnp.bfloat16),
            pltpu.VMEM((groups * tok, 2 * tok), jnp.bfloat16),
        ],
        compiler_params=params,
        cost_estimate=pl.CostEstimate(
            flops=40 * 8 * groups * tok * 2 * tok * width, bytes_accessed=12 * 2**20,
            transcendentals=0,
        ),
        name="conv",
    )(inverse, doc_ids, by_channel, long, docs[:, None])
    with jax.named_scope("back_to_tokens"):
        conv, attended = lax.optimization_barrier((conv, exchange(attended)))
        summed = featured[:, 0] * as_tokens(exchange(conv)) + as_tokens(attended)
    row_squares = lax.psum(jnp.sum(summed * summed, axis=1), "mp")
    norm_scale = lax.rsqrt(row_squares / (chl * lax.axis_size("mp")) + 1e-05)
    return summed * norm_scale[:, None] * norm_gain[None, :]


def fits(tok, chl, groups_l, se_len, mr_len, count):
    return (
        chl == count * HD
        and groups_l % count == 0
        and TILE % tok == 0
        and tok >= 128
        and (count * tok) % TILE == 0
        and mr_len <= tok
        and se_len <= 9
    )


def per_device(*args):
    streams, se_filter, mr_filter = args[:3]
    sizes = (streams.shape[0], streams.shape[2], se_filter.shape[2])
    if fits(*sizes, se_filter.shape[0], mr_filter.shape[0], args[7].shape[0]):
        return split_heads(*args)
    return gather_all(*args)


def gather_all(
    streams, se_filter, mr_filter, mr_decay, query, key, value, placement_list, doc_ids, norm_gain
):
    tok = streams.shape[0]
    chl = streams.shape[2]
    groups_l = se_filter.shape[2]
    group_w = chl // groups_l
    se_len = se_filter.shape[0]
    mr_len = mr_filter.shape[0]
    heads_l = chl // HD
    seq_count = placement_list.shape[0]
    device = lax.axis_index("seq")
    stretch = placement_list[device]
    listing = jnp.arange(seq_count, dtype=jnp.int32)
    source = jnp.sum(jnp.where(placement_list == stretch - 1, listing, 0))
    base = stretch * tok
    offsets = jnp.arange(tok, dtype=jnp.int32)
    local_pos = base + offsets
    local_doc = lax.dynamic_slice_in_dim(doc_ids, base, tok)

    def earlier_docs(width):
        where_pos = base - width + jnp.arange(width, dtype=jnp.int32)
        found = doc_ids[jnp.clip(where_pos, 0, doc_ids.shape[0] - 1)]
        return jnp.where(where_pos >= 0, found, -1)

    def pick(piece):
        owner = jnp.arange(piece.shape[0], dtype=jnp.int32) == source
        mask = owner.reshape((piece.shape[0],) + (1,) * (piece.ndim - 1))
        return jnp.sum(jnp.where(mask, piece, 0.0), axis=0)

    short_tail = pick(
        lax.all_gather(streams[tok - (se_len - 1) :][None], "seq", axis=0, tiled=True)
    )
    extended = jnp.concatenate([short_tail, streams], axis=0)
    ext_doc = jnp.concatenate([earlier_docs(se_len - 1), local_doc])
    short_taps = jnp.repeat(se_filter, group_w, axis=2)
    featured = jnp.zeros((tok, 3, chl), jnp.float32)
    for lag in range(se_len):
        first = se_len - 1 - lag
        same = (ext_doc[first : first + tok] == local_doc)[:, None, None]
        featured = featured + jnp.where(
            same, short_taps[lag][None] * extended[first : first + tok], 0.0
        )
    gated = featured[:, 1] * featured[:, 2]
    decays = jnp.arange(mr_len, dtype=jnp.float32)[:, None]
    taps = mr_filter * jnp.exp(-mr_decay[None, :] * decays)
    scale = 1.0 / jnp.sqrt(jnp.float32(HD))
    tail_piece = gated[tok - (mr_len - 1) :][None]
    long_tail = pick(lax.all_gather(tail_piece, "seq", axis=0, tiled=True))
    q_heads = query.reshape(tok, heads_l, HD)
    key_pos = (placement_list[:, None] * tok + offsets[None, :]).reshape(-1)
    key_doc = doc_ids[jnp.clip(key_pos, 0, doc_ids.shape[0] - 1)]
    allowed = (
        (key_pos >= 0)[None, :]
        & (key_pos[None, :] <= local_pos[:, None])
        & (key_doc[None, :] == local_doc[:, None])
    )[None]
    k_heads = lax.all_gather(key[None], "seq", axis=0, tiled=True).reshape(-1, heads_l, HD)
    v_heads = lax.all_gather(value[None], "seq", axis=0, tiled=True).reshape(-1, heads_l, HD)
    top_old = jnp.full((heads_l, tok), -1e30, jnp.float32)
    scores = jnp.einsum("qhd,khd->hqk", q_heads, k_heads, precision=lax.Precision.HIGHEST) * scale
    scores = jnp.where(allowed, scores, jnp.float32(-1e30))
    top_new = jnp.maximum(top_old, jnp.max(scores, axis=2))
    weights = jnp.where(allowed, jnp.exp(scores - top_new[:, :, None]), 0.0)
    total_new = jnp.sum(weights, axis=2)
    acc_new = jnp.einsum("hqk,khd->hqd", weights, v_heads, precision=lax.Precision.HIGHEST)
    attended = (acc_new / total_new[:, :, None]).transpose(1, 0, 2).reshape(tok, chl)
    span = tok + mr_len - 1
    ext_rows = jnp.concatenate([long_tail, gated], axis=0)
    doc_rows = jnp.concatenate([earlier_docs(mr_len - 1), local_doc])
    lag = (
        jnp.arange(tok, dtype=jnp.int32)[:, None]
        + (mr_len - 1)
        - jnp.arange(span, dtype=jnp.int32)[None, :]
    )
    valid = (lag >= 0) & (lag < mr_len) & (doc_rows[None, :] == local_doc[:, None])
    toeplitz = jnp.where(valid[:, :, None], taps[jnp.clip(lag, 0, mr_len - 1)], 0.0)
    conv = jnp.einsum(
        "tsg,sgc->tgc",
        toeplitz,
        ext_rows.reshape(span, groups_l, group_w),
        precision=lax.Precision.HIGHEST,
    ).reshape(tok, chl)
    hyena = featured[:, 0] * conv
    summed = hyena + attended
    row_squares = lax.psum(jnp.sum(summed * summed, axis=1), "mp")
    norm_scale = lax.rsqrt(row_squares / (chl * lax.axis_size("mp")) + 1e-05)
    return summed * norm_scale[:, None] * norm_gain[None, :]


def solution(mesh):
    placed = (
        P("seq", None, "mp"),
        P(None, None, "mp"),
        P(None, "mp"),
        P("mp"),
        P("seq", "mp"),
        P("seq", "mp"),
        P("seq", "mp"),
        P(),
        P(),
        P("mp"),
    )
    return jax.shard_map(
        per_device, mesh=mesh, in_specs=placed, out_specs=P("seq", "mp"), check_vma=False
    )
```

```python
import functools

import jax
import jax.numpy as jnp
from jax import lax
from jax.experimental import pallas as pl
from jax.experimental.pallas import tpu as pltpu
from jax.sharding import PartitionSpec as P

HD = 128
TILE = 256
NT = (((1,), (1,)), ((), ()))


def halves(x):
    high = x.astype(jnp.bfloat16)
    return high, (x - high.astype(jnp.float32)).astype(jnp.bfloat16)


def mul(a, b):
    return jnp.dot(a, b, preferred_element_type=jnp.float32)


def conv_kernel(
    group_w, inv_ref, doc_ref, packed_ref, short_ref, long_ref, docs_ref, place_ref, out_ref,
    ext, window, long_hi, long_lo,
):
    count, tok, width = out_ref.shape
    lags, kinds, _ = short_ref.shape
    lead = ext.shape[1] // 2
    inner = tok - lead
    groups = width // group_w
    long_hi[...], long_lo[...] = halves(long_ref[...])
    window[...] = jnp.zeros_like(window)
    lane_group = lax.broadcasted_iota(jnp.int32, (tok, width), 1) // group_w

    def stretch(c, carry):
        b = inv_ref[c]
        before = inv_ref[jnp.maximum(c - 1, 0)]
        place = place_ref[pl.ds(pl.multiple_of(c * tok, tok), lead), :]
        edge = []
        for j in range(kinds):
            tail, first = inner + j * lead, inner + (kinds + j) * lead
            ext[j, :lead] = packed_ref[before, tail : tail + lead]
            ext[j, lead:] = packed_ref[b, first : first + lead]
            total = short_ref[0, j][None, :] * ext[j, lead:]
            for lag in range(1, lags):
                term = short_ref[lag, j][None, :] * ext[j, lead - lag : 2 * lead - lag]
                total = total + jnp.where(place >= lag, term, 0.0)
            edge.append(total)
        window[:tok] = window[tok:]
        window[tok : tok + lead] = edge[1] * edge[2]
        window[tok + lead :] = packed_ref[b, :inner]
        docs = docs_ref[pl.ds(pl.multiple_of(c * tok, tok), 2 * tok), :]

        def document(d, conv):
            hi, lo = halves(jnp.where(docs == d, window[...], 0.0))
            both = mul(long_hi[...], jnp.concatenate([hi, lo], axis=1))
            full = both[:, :width] + both[:, width:] + mul(long_lo[...], hi)
            part = jnp.zeros((tok, width), jnp.float32)
            for g in range(groups):
                part = jnp.where(lane_group == g, full[g * tok : (g + 1) * tok], part)
            return jnp.where(docs[tok:] == d, part, conv)

        conv = lax.fori_loop(
            doc_ref[c * tok],
            doc_ref[c * tok + tok - 1] + 1,
            document,
            jnp.zeros((tok, width), jnp.float32),
        )
        out_ref[b, :lead] = edge[0] * conv[:lead]
        out_ref[b, lead:] = conv[lead:]
        return carry

    lax.fori_loop(0, count, stretch, 0)


def attention_kernel(
    scale, inv_ref, start_ref, q_ref, kv_ref, starts_ref, out_ref, keys, values
):
    count, tok, width = q_ref.shape
    per = TILE // tok

    def prepare(c, carry):
        rows = pl.ds(pl.multiple_of(c * tok, tok), tok)
        b = inv_ref[c]
        keys[rows, :] = jnp.concatenate(halves(kv_ref[b, 0]), axis=1)
        values[rows, :] = jnp.concatenate(halves(kv_ref[b, 1]), axis=1)
        return carry

    lax.fori_loop(0, count, prepare, 0)

    def rows_of(i, carry):
        stored = [inv_ref[i * per + r] for r in range(per)]
        q = jnp.concatenate([q_ref[b] for b in stored], axis=0) * scale
        q_hi, q_lo = halves(q)
        q_both = jnp.concatenate([q_hi, q_hi], axis=1)
        starts = starts_ref[pl.ds(pl.multiple_of(i * TILE, TILE), TILE), :]
        row = i * TILE + lax.broadcasted_iota(jnp.int32, (TILE, TILE), 0)
        lane = lax.broadcasted_iota(jnp.int32, (TILE, TILE), 1)

        def block(j, carry):
            top, total, acc = carry
            rows = pl.ds(pl.multiple_of(j * TILE, TILE), TILE)
            k = keys[rows, :]
            s = lax.dot_general(q_both, k, NT, preferred_element_type=jnp.float32)
            s = s + lax.dot_general(q_lo, k[:, :width], NT, preferred_element_type=jnp.float32)
            col = j * TILE + lane
            allowed = (col >= starts) & (col <= row)
            s = jnp.where(allowed, s, -1e30)
            new = jnp.maximum(top, jnp.max(s, axis=1, keepdims=True))
            w = jnp.where(allowed, jnp.exp(s - new), 0.0)
            fade = jnp.exp(top - new)
            w_hi, w_lo = halves(w)
            v = values[rows, :]
            both = mul(w_hi, v)
            got = both[:, :width] + both[:, width:] + mul(w_lo, v[:, :width])
            return new, fade * total + jnp.sum(w, axis=1, keepdims=True), fade * acc + got

        first = lax.div(start_ref[i * TILE], TILE)
        top, total, acc = lax.fori_loop(
            first,
            i + 1,
            block,
            (
                jnp.full((TILE, 1), -1e30, jnp.float32),
                jnp.zeros((TILE, 1), jnp.float32),
                jnp.zeros((TILE, width), jnp.float32),
            ),
        )
        attended = acc / total
        for r, b in enumerate(stored):
            out_ref[b] = attended[r * tok : (r + 1) * tok]
        return carry

    lax.fori_loop(0, count // per, rows_of, 0)


def split_heads(
    streams, se_filter, mr_filter, mr_decay, query, key, value, placement_list, doc_ids, norm_gain
):
    tok, kinds, chl = streams.shape
    se_len, _, groups_l = se_filter.shape
    mr_len = mr_filter.shape[0]
    count = placement_list.shape[0]
    group_w = chl // groups_l
    width = chl // count
    groups = groups_l // count
    tokens = count * tok
    me = lax.axis_index("seq")
    index = jnp.arange(count, dtype=jnp.int32)
    inverse = jnp.sum(
        jnp.where(placement_list[None, :] == index[:, None], index[None, :], 0), axis=1
    )
    positions = jnp.arange(tokens, dtype=jnp.int32)
    fresh = jnp.concatenate([jnp.ones((1,), bool), doc_ids[1:] != doc_ids[:-1]])
    starts = lax.cummax(jnp.where(fresh, positions, 0))
    docs = jnp.concatenate([jnp.full((tok,), -1, jnp.int32), doc_ids])

    def exchange(x):
        return lax.all_to_all(x, "seq", 0, 0, tiled=True)

    def as_tokens(x):
        return x.transpose(1, 0, 2).reshape(-1, chl)

    lead = -(-(se_len - 1) // 8) * 8
    stretch = placement_list[me]
    places = positions - starts

    def by_block(x):
        return x.reshape(-1, count, width).transpose(1, 0, 2)

    with jax.named_scope("query_to_heads"):
        q_head = exchange(by_block(query))
    with jax.named_scope("key_value_to_heads"):
        place = lax.dynamic_slice_in_dim(places, stretch * tok, tok)[lead:]
        sent = jnp.stack([by_block(key), by_block(value)], axis=1)
        sent, q_head, place = lax.optimization_barrier((sent, q_head, place))
        kv_head = exchange(sent)
    with jax.named_scope("featured"):
        short = jnp.repeat(se_filter, group_w, axis=2)
        featured = short[0][None] * streams[lead:]
        for lag in range(1, se_len):
            term = short[lag][None] * streams[lead - lag : tok - lag]
            featured = featured + jnp.where((place >= lag)[:, None, None], term, 0.0)
        gated = featured[:, 1] * featured[:, 2]
    with jax.named_scope("gated_to_channels"):
        ends = [streams[tok - lead :, j] for j in range(kinds)]
        ends += [streams[:lead, j] for j in range(kinds)]
        packed = by_block(jnp.concatenate([gated] + ends, axis=0))
        sent, kv_head = lax.optimization_barrier((packed, kv_head))
        by_channel = exchange(sent)

    with jax.named_scope("filters"):
        short = lax.dynamic_slice_in_dim(se_filter, me * groups, groups, 2)
        short = jnp.repeat(short, group_w, axis=2)
        decays = jnp.arange(mr_len, dtype=jnp.float32)[:, None]
        taps = lax.dynamic_slice_in_dim(mr_filter, me * groups, groups, 1)
        decay = lax.dynamic_slice_in_dim(mr_decay, me * groups, groups, 0)
        taps = (taps * jnp.exp(-decay[None, :] * decays)).T
        period = 3 * tok
        line = jnp.concatenate(
            [
                jnp.zeros((groups, tok - mr_len + 1), jnp.float32),
                taps[:, ::-1],
                jnp.zeros((groups, period - tok - 1), jnp.float32),
            ],
            axis=1,
        )
        sheared = jnp.tile(line, (1, tok))[:, : tok * (period - 1)]
        long = sheared.reshape(groups, tok, period - 1)[:, :, : 2 * tok]
        long = long.reshape(groups * tok, 2 * tok)

    smem = pl.BlockSpec(memory_space=pltpu.SMEM)
    vmem = pl.BlockSpec(memory_space=pltpu.VMEM)
    shape = jax.ShapeDtypeStruct((count, tok, width), jnp.float32)
    params = pltpu.CompilerParams(vmem_limit_bytes=56 * 2**20)
    attended = pl.pallas_call(
        functools.partial(attention_kernel, 1.0 / HD**0.5),
        out_shape=shape,
        in_specs=[smem, smem, vmem, vmem, vmem],
        out_specs=vmem,
        scratch_shapes=[
            pltpu.VMEM((tokens, 2 * width), jnp.bfloat16),
            pltpu.VMEM((tokens, 2 * width), jnp.bfloat16),
        ],
        compiler_params=params,
        cost_estimate=pl.CostEstimate(
            flops=40 * tokens * 1024 * width, bytes_accessed=12 * 2**20,
            transcendentals=tokens * 1024,
        ),
        name="attention",
    )(inverse, starts, q_head, kv_head, starts[:, None])
    by_channel, attended = lax.optimization_barrier((by_channel, attended))
    conv = pl.pallas_call(
        functools.partial(conv_kernel, group_w),
        out_shape=shape,
        in_specs=[smem, smem, vmem, vmem, vmem, vmem, vmem],
        out_specs=vmem,
        scratch_shapes=[
            pltpu.VMEM((kinds, 2 * lead, width), jnp.float32),
            pltpu.VMEM((2 * tok, width), jnp.float32),
            pltpu.VMEM((groups * tok, 2 * tok), jnp.bfloat16),
            pltpu.VMEM((groups * tok, 2 * tok), jnp.bfloat16),
        ],
        compiler_params=params,
        cost_estimate=pl.CostEstimate(
            flops=40 * 8 * groups * tok * 2 * tok * width, bytes_accessed=12 * 2**20,
            transcendentals=0,
        ),
        name="conv",
    )(inverse, doc_ids, by_channel, short, long, docs[:, None], places[:, None])
    with jax.named_scope("back_to_tokens"):
        conv, attended = lax.optimization_barrier((conv, exchange(attended)))
        outer = jnp.concatenate([jnp.ones((lead, chl), jnp.float32), featured[:, 0]], axis=0)
        summed = outer * as_tokens(exchange(conv)) + as_tokens(attended)
    row_squares = lax.psum(jnp.sum(summed * summed, axis=1), "mp")
    norm_scale = lax.rsqrt(row_squares / (chl * lax.axis_size("mp")) + 1e-05)
    return summed * norm_scale[:, None] * norm_gain[None, :]


def fits(tok, chl, groups_l, se_len, mr_len, count):
    return (
        chl == count * HD
        and groups_l % count == 0
        and TILE % tok == 0
        and tok >= 128
        and (count * tok) % TILE == 0
        and mr_len <= tok
        and se_len <= 9
    )


def per_device(*args):
    streams, se_filter, mr_filter = args[:3]
    sizes = (streams.shape[0], streams.shape[2], se_filter.shape[2])
    if fits(*sizes, se_filter.shape[0], mr_filter.shape[0], args[7].shape[0]):
        return split_heads(*args)
    return gather_all(*args)


def gather_all(
    streams, se_filter, mr_filter, mr_decay, query, key, value, placement_list, doc_ids, norm_gain
):
    tok = streams.shape[0]
    chl = streams.shape[2]
    groups_l = se_filter.shape[2]
    group_w = chl // groups_l
    se_len = se_filter.shape[0]
    mr_len = mr_filter.shape[0]
    heads_l = chl // HD
    seq_count = placement_list.shape[0]
    device = lax.axis_index("seq")
    stretch = placement_list[device]
    listing = jnp.arange(seq_count, dtype=jnp.int32)
    source = jnp.sum(jnp.where(placement_list == stretch - 1, listing, 0))
    base = stretch * tok
    offsets = jnp.arange(tok, dtype=jnp.int32)
    local_pos = base + offsets
    local_doc = lax.dynamic_slice_in_dim(doc_ids, base, tok)

    def earlier_docs(width):
        where_pos = base - width + jnp.arange(width, dtype=jnp.int32)
        found = doc_ids[jnp.clip(where_pos, 0, doc_ids.shape[0] - 1)]
        return jnp.where(where_pos >= 0, found, -1)

    def pick(piece):
        owner = jnp.arange(piece.shape[0], dtype=jnp.int32) == source
        mask = owner.reshape((piece.shape[0],) + (1,) * (piece.ndim - 1))
        return jnp.sum(jnp.where(mask, piece, 0.0), axis=0)

    short_tail = pick(
        lax.all_gather(streams[tok - (se_len - 1) :][None], "seq", axis=0, tiled=True)
    )
    extended = jnp.concatenate([short_tail, streams], axis=0)
    ext_doc = jnp.concatenate([earlier_docs(se_len - 1), local_doc])
    short_taps = jnp.repeat(se_filter, group_w, axis=2)
    featured = jnp.zeros((tok, 3, chl), jnp.float32)
    for lag in range(se_len):
        first = se_len - 1 - lag
        same = (ext_doc[first : first + tok] == local_doc)[:, None, None]
        featured = featured + jnp.where(
            same, short_taps[lag][None] * extended[first : first + tok], 0.0
        )
    gated = featured[:, 1] * featured[:, 2]
    decays = jnp.arange(mr_len, dtype=jnp.float32)[:, None]
    taps = mr_filter * jnp.exp(-mr_decay[None, :] * decays)
    scale = 1.0 / jnp.sqrt(jnp.float32(HD))
    tail_piece = gated[tok - (mr_len - 1) :][None]
    long_tail = pick(lax.all_gather(tail_piece, "seq", axis=0, tiled=True))
    q_heads = query.reshape(tok, heads_l, HD)
    key_pos = (placement_list[:, None] * tok + offsets[None, :]).reshape(-1)
    key_doc = doc_ids[jnp.clip(key_pos, 0, doc_ids.shape[0] - 1)]
    allowed = (
        (key_pos >= 0)[None, :]
        & (key_pos[None, :] <= local_pos[:, None])
        & (key_doc[None, :] == local_doc[:, None])
    )[None]
    k_heads = lax.all_gather(key[None], "seq", axis=0, tiled=True).reshape(-1, heads_l, HD)
    v_heads = lax.all_gather(value[None], "seq", axis=0, tiled=True).reshape(-1, heads_l, HD)
    top_old = jnp.full((heads_l, tok), -1e30, jnp.float32)
    scores = jnp.einsum("qhd,khd->hqk", q_heads, k_heads, precision=lax.Precision.HIGHEST) * scale
    scores = jnp.where(allowed, scores, jnp.float32(-1e30))
    top_new = jnp.maximum(top_old, jnp.max(scores, axis=2))
    weights = jnp.where(allowed, jnp.exp(scores - top_new[:, :, None]), 0.0)
    total_new = jnp.sum(weights, axis=2)
    acc_new = jnp.einsum("hqk,khd->hqd", weights, v_heads, precision=lax.Precision.HIGHEST)
    attended = (acc_new / total_new[:, :, None]).transpose(1, 0, 2).reshape(tok, chl)
    span = tok + mr_len - 1
    ext_rows = jnp.concatenate([long_tail, gated], axis=0)
    doc_rows = jnp.concatenate([earlier_docs(mr_len - 1), local_doc])
    lag = (
        jnp.arange(tok, dtype=jnp.int32)[:, None]
        + (mr_len - 1)
        - jnp.arange(span, dtype=jnp.int32)[None, :]
    )
    valid = (lag >= 0) & (lag < mr_len) & (doc_rows[None, :] == local_doc[:, None])
    toeplitz = jnp.where(valid[:, :, None], taps[jnp.clip(lag, 0, mr_len - 1)], 0.0)
    conv = jnp.einsum(
        "tsg,sgc->tgc",
        toeplitz,
        ext_rows.reshape(span, groups_l, group_w),
        precision=lax.Precision.HIGHEST,
    ).reshape(tok, chl)
    hyena = featured[:, 0] * conv
    summed = hyena + attended
    row_squares = lax.psum(jnp.sum(summed * summed, axis=1), "mp")
    norm_scale = lax.rsqrt(row_squares / (chl * lax.axis_size("mp")) + 1e-05)
    return summed * norm_scale[:, None] * norm_gain[None, :]


def solution(mesh):
    placed = (
        P("seq", None, "mp"),
        P(None, None, "mp"),
        P(None, "mp"),
        P("mp"),
        P("seq", "mp"),
        P("seq", "mp"),
        P("seq", "mp"),
        P(),
        P(),
        P("mp"),
    )
    return jax.shard_map(
        per_device, mesh=mesh, in_specs=placed, out_specs=P("seq", "mp"), check_vma=False
    )
```
